32 devices in a mesh: gx: 4 (over z), gy: 8 (over y, x, core).
Axes of the slice: x: 2, y: 2, z: 4, core: 2. Of those that a mesh axis runs over, the one named last changes fastest.
Arguments:
- queries: bfloat16 [1024, 4096], P('gy', 'gx'), may hold values from -8 to 8
- new_kv: bfloat16 [1024, 8, 128], P('gy', 'gx'), may hold values from -8 to 8
- kv_cache: bfloat16 [4096, 8, 128], P('gy', 'gx'), may hold values from -8 to 8
- cache_seg: int32 [4096], P('gy'), may hold values from -1 to 15, as said below
- cache_slot: int32 [1024], P('gy'), may hold values from 0 to 4095, as said below
- token_seg: int32 [1024], P('gy'), may hold values from 0 to 15, never falling along the last dimension, each value on 1 to 512 neighbouring positions
- pad_mask: int32 [1024], P('gy'), may hold values 0 or 1
- sink_logits: float32 [64], P('gx'), may hold values from 0 to 4
- out_weight: bfloat16 [4096, 2880], P('gx', 'gy'), may hold values from -0.75 to 0.75
- out_bias: float32 [2880], P('gx'), may hold values from -2 to 2
Outputs:
- attended: bfloat16 [1024, 2880], P('gy', 'gx')
- cache_out: bfloat16 [4096, 8, 128], P('gy', 'gx')
The draws below stay inside these ranges and needn't reach their ends.
Inputs may be any that keep to these rules, and one draw needn't show every extreme that they name: `cache_seg`: the sequence whose cached key and value a slot holds, or -1 for an empty slot. Distinct slots, each empty (-1) in cache_seg; cache_slot[t] // 512 == t // 128.
All inputs are finite; a program needn't handle non-finite values. No bound on the sum of `pad_mask` on one device may be relied on, other than what follows from the above.
Results may differ from the reference program's by a relative error of at most 0.015.
Values may be sent and summed in bfloat16 or wider, within the bound.
No kernel may reach another device: no remote copies, remote signals or barrier semaphores. Data moves between devices by JAX's collectives and lax.ppermute only.
A program may use at most 128 MiB of HBM per device.

```python
import math
import jax
import jax.numpy as jnp
import numpy as np
from jax import lax

D = 2880
HEADS = 64
KVH = 8
HD = 64
TOK_DEV = 128
CACHE_DEV = 512
NSEG = 16
TOKENS = 1024
CACHE = 4096
LONG = 512


def draw_queries(key, part):
    values = jax.random.truncated_normal(jax.random.fold_in(key, 11), -8.0, 8.0, (TOKENS, HEADS, HD), jnp.float32)
    return values.reshape(TOKENS, HEADS * HD).astype(jnp.bfloat16)


def draw_new_kv(key, part):
    values = jax.random.truncated_normal(jax.random.fold_in(key, 13), -8.0, 8.0, (TOKENS, KVH, 2 * HD), jnp.float32)
    return values.astype(jnp.bfloat16)


def slot_perms(key):
    shard_count = CACHE // CACHE_DEV
    base = jax.random.fold_in(key, 202)
    shard_keys = jax.random.split(base, shard_count)
    return jax.vmap(lambda one_key: jax.random.permutation(one_key, CACHE_DEV))(shard_keys).astype(jnp.int32)


def draw_cache_slot(key, part):
    shard_count = CACHE // CACHE_DEV
    perms = slot_perms(key)
    offsets = jnp.arange(shard_count, dtype=jnp.int32)[:, None] * CACHE_DEV
    return (perms[:, :TOK_DEV] + offsets).reshape(TOKENS).astype(jnp.int32)


def draw_cache_seg(key, part):
    shard_count = CACHE // CACHE_DEV
    perms = slot_perms(key)
    ranks = jnp.argsort(perms, axis=1, stable=True)
    writes = ranks < TOK_DEV
    first_owner = jax.random.randint(jax.random.fold_in(key, 205), (shard_count, CACHE_DEV), 0, NSEG)
    second_owner = jax.random.randint(jax.random.fold_in(key, 206), (shard_count, CACHE_DEV), 0, NSEG)
    owner = jnp.minimum(first_owner, second_owner)
    empty = jax.random.randint(jax.random.fold_in(key, 207), (shard_count, CACHE_DEV), 0, 8) == 0
    return jnp.where(writes | empty, -1, owner).reshape(CACHE).astype(jnp.int32)


def touch_ends(result, key, smallest, top_value):
    place = [jax.random.randint(jax.random.fold_in(key, axis), (), 0, length) for axis, length in enumerate(result.shape)]
    longest = result.shape.index(max(result.shape))
    next_to = place[:longest] + [(place[longest] + 1) % result.shape[longest]] + place[longest + 1:]
    return result.at[tuple(place)].set(smallest).at[tuple(next_to)].set(top_value)


def levels(key, dims, cuts, least, largest):
    loudness, own = 1.0, jax.random.fold_in(key, 6)
    for position, shards_of in cuts:
        draws = jnp.exp(jax.random.uniform(jax.random.fold_in(own, position), (shards_of,), jnp.float32, least / len(cuts), largest / len(cuts)))
        loudness = loudness * jnp.repeat(draws, dims[position] // shards_of).reshape([-1 if axis == position else 1 for axis in range(len(dims))])
    return loudness


def split_up(number_of, total, reach, lean):
    weights = [(1 << 20) // math.isqrt(grade ** lean) + 1 for grade in range(2, number_of + 1)]
    spare, counts = total - reach - (number_of - 1), [1] * (number_of - 1)
    while spare > 0:
        free = [i for i in range(number_of - 1) if counts[i] < reach]
        pool, remaining = sum([weights[i] for i in free]), spare
        for i in free:
            addition = min(reach - counts[i], max(1, remaining * weights[i] // pool), spare)
            counts[i] = counts[i] + addition
            spare = spare - addition
    return np.array([reach] + counts)


def ragged(rng, count, total, reach, skew):
    if count == 2:
        one = jax.random.randint(rng, (), max(1, total - reach), min(reach, total - 1) + 1)
        return jnp.stack([one, total - one])
    lengths = jnp.asarray(split_up(count, total, reach, skew), jnp.int32)
    pairs = (count - 1) // 2
    giver, sink = lengths[1:1 + 2 * pairs:2], lengths[2:2 + 2 * pairs:2]
    room = jnp.minimum(giver - 1, reach - sink)
    moved = jax.random.randint(jax.random.fold_in(rng, 1), (pairs,), 0, 1 << 20) % (room + 1)
    lengths = lengths.at[1:1 + 2 * pairs:2].set(giver - moved).at[2:2 + 2 * pairs:2].set(sink + moved)
    return lengths[jax.random.permutation(jax.random.fold_in(rng, 2), count)]


def noise(key, shape, scale, reach, cuts=(), held_as=jnp.bfloat16):
    values = jax.random.normal(key, shape, jnp.float32) * scale
    if len(cuts) > 0:
        values = levels(key, shape, cuts, -0.22, 0.18) * values
    return jnp.clip(values, min=-reach, max=reach).astype(held_as)


def setup_inputs(seed: int = 0) -> dict:
    streams_of = jax.random.split(jax.random.key(seed), 11)
    queries = draw_queries(jax.random.fold_in(streams_of[10], 71), 0)
    new_kv = draw_new_kv(jax.random.fold_in(streams_of[10], 71), 0)
    kv_cache = noise(streams_of[2], (CACHE, KVH, 2 * HD), 1.0, 8.0, ((0, 8), (1, 4)))
    cache_seg = draw_cache_seg(jax.random.fold_in(streams_of[10], 71), 0)
    cache_slot = draw_cache_slot(jax.random.fold_in(streams_of[10], 71), 0)
    token_seg = jnp.searchsorted(jnp.cumsum(ragged(streams_of[5], NSEG, TOKENS, LONG, 2)), jnp.arange(TOKENS), side="right").astype(jnp.int32)
    pad_mask = touch_ends((jax.random.randint(streams_of[6], (TOKENS,), 0, 16) < 15).astype(jnp.int32), jax.random.fold_in(streams_of[6], 1), 0, 1)
    sink_logits = jnp.clip(4.0 * jax.random.uniform(streams_of[7], (HEADS,), jnp.float32) ** levels(streams_of[7], (HEADS,), ((0, 4),), -0.2, 0.2), 0.0, 4.0)
    out_weight = noise(streams_of[8], (HEADS * HD, D), HD ** -0.5, 0.75, ((0, 4), (1, 8)))
    out_bias = noise(streams_of[9], (D,), 0.3, 2.0, ((0, 4),), jnp.float32)
    return dict(queries=queries, new_kv=new_kv, kv_cache=kv_cache, cache_seg=cache_seg, cache_slot=cache_slot, token_seg=token_seg, pad_mask=pad_mask, sink_logits=sink_logits, out_weight=out_weight, out_bias=out_bias)


def reference(queries, new_kv, kv_cache, cache_seg, cache_slot, token_seg, pad_mask, sink_logits, out_weight, out_bias):
    live_rows = pad_mask == 1
    target = jnp.where(live_rows, cache_slot, CACHE).astype(jnp.int32)
    cache_out = kv_cache.at[target].set(new_kv, mode="drop")
    slot_seg = cache_seg.at[target].set(token_seg, mode="drop")
    token_index = jnp.arange(TOKENS, dtype=jnp.int32)
    slot_order = jnp.full((CACHE,), -1, jnp.int32).at[target].set(token_index, mode="drop")
    group_heads = HEADS // KVH
    scale = HD ** -0.5
    keys_all = jnp.transpose(cache_out[:, :, :HD].astype(jnp.float32), (1, 0, 2))
    values_all = jnp.transpose(cache_out[:, :, HD:].astype(jnp.float32), (1, 0, 2))
    query_heads = queries.astype(jnp.float32).reshape(TOKENS, KVH, group_heads, HD)
    sink_table = sink_logits.reshape(KVH, group_heads)
    row_block = math.gcd(TOKENS, 256)

    def one_block(row_start):
        block_queries = lax.dynamic_slice_in_dim(query_heads, row_start, row_block, 0)
        block_seg = lax.dynamic_slice_in_dim(token_seg, row_start, row_block, 0)
        block_index = row_start + jnp.arange(row_block, dtype=jnp.int32)
        visible = (slot_seg[None, :] == block_seg[:, None]) & (slot_order[None, :] <= block_index[:, None])

        def one_group(group_data):
            grp_queries, grp_keys, grp_values, grp_sink = group_data
            scores = jnp.einsum("tqd,cd->qtc", grp_queries, grp_keys) * scale
            sink_col = grp_sink[:, None]
            peak = jnp.maximum(sink_col, jnp.max(jnp.where(visible[None], scores, -jnp.inf), axis=-1))
            weights = jnp.where(visible[None], jnp.exp(scores - peak[..., None]), 0.0)
            rounded = lax.optimization_barrier(weights.astype(jnp.bfloat16)).astype(jnp.float32)
            numerator = jnp.einsum("qtc,cd->tqd", rounded, grp_values)
            denominator = jnp.exp(sink_col - peak) + jnp.sum(weights, axis=-1)
            return numerator / jnp.transpose(denominator)[:, :, None]

        grouped = lax.map(one_group, (jnp.transpose(block_queries, (1, 0, 2, 3)), keys_all, values_all, sink_table))
        return jnp.transpose(grouped, (1, 0, 2, 3)).reshape(row_block, HEADS * HD)

    starts = jnp.arange(TOKENS // row_block, dtype=jnp.int32) * row_block
    blocks = lax.map(one_block, starts).reshape(TOKENS, HEADS * HD)
    attention = (blocks * pad_mask[:, None].astype(jnp.float32)).astype(jnp.bfloat16)
    projected = jnp.dot(attention, out_weight, preferred_element_type=jnp.float32) + out_bias
    return projected.astype(jnp.bfloat16), cache_out
```

```python
import functools
import math

import jax
import jax.numpy as jnp
from jax import lax
from jax.experimental import pallas as pl
from jax.experimental.pallas import tpu as pltpu
from jax.sharding import PartitionSpec as P

F32 = jnp.float32
BF16 = jnp.bfloat16
HIDE = -1e30
VMEM = pl.BlockSpec(memory_space=pltpu.VMEM)
SMEM = pl.BlockSpec(memory_space=pltpu.SMEM)


def iota(shape, dim):
    return lax.broadcasted_iota(jnp.int32, shape, dim)


def to_column(row):
    n = row.shape[1]
    eye = iota((n, n), 0) == iota((n, n), 1)
    return jnp.sum(jnp.where(eye, row, 0.0), axis=1, keepdims=True)


def dot_nt(a, b):
    return lax.dot_general(a, b, (((1,), (1,)), ((), ())), preferred_element_type=F32)


def prep_kernel(base_ref, kv_ref, new_ref, cseg_ref, slot_ref, tseg_ref, pad_ref, cache_ref, rows_ref):
    slots, tokens = kv_ref.shape[0], new_ref.shape[0]
    groups = kv_ref.shape[1] // 128
    target = jnp.where(pad_ref[...] == 1, slot_ref[...] - base_ref[0], -1).astype(F32)
    place = (iota((slots, tokens), 0).astype(F32) == target).astype(BF16)
    moved = jnp.dot(place, new_ref[...], preferred_element_type=F32)
    written = jnp.dot(place, jnp.ones((tokens, 128), BF16), preferred_element_type=F32)
    written = jnp.concatenate([written] * groups, axis=1)
    cache = jnp.where(written > 0.5, moved, kv_ref[...].astype(F32)).astype(BF16)
    cache_ref[...] = cache

    back = to_column(target) == iota((tokens, slots), 1).astype(F32)
    order = jnp.sum(jnp.where(back, (iota((tokens, slots), 0) + 1).astype(F32), 0.0), axis=0, keepdims=True) - 1.0
    new_seg = jnp.sum(jnp.where(back, to_column(tseg_ref[...].astype(F32)), 0.0), axis=0, keepdims=True)
    seg = jnp.where(order >= 0.0, new_seg, cseg_ref[...].astype(F32))
    lane = iota((1, slots), 1).astype(F32)
    key = jnp.where(seg < 0.0, 64.0, seg) * slots + lane
    rank = jnp.sum(jnp.where(to_column(key) < key, 1.0, 0.0), axis=0, keepdims=True)
    perm = (iota((slots, slots), 0).astype(F32) == rank).astype(BF16)
    rows = jnp.dot(perm, cache, preferred_element_type=F32).astype(BF16)
    for g in range(groups):
        rows_ref[g * slots : (g + 1) * slots, :] = rows[:, g * 128 : (g + 1) * 128]
    sub = iota((8, slots), 0)
    labels = jnp.where(sub == 0, seg, jnp.where(sub == 1, order, 0.0)).astype(BF16)
    labels = dot_nt(labels, perm)
    parts = [labels[r : r + 1, c : c + 128] for r in range(2) for c in range(0, slots, 128)]
    parts.append(jnp.zeros((16 - len(parts), 128), F32))
    rows_ref[groups * slots :, :] = jnp.concatenate(parts, axis=0).astype(BF16)


def attend_kernel(first, last, count, *refs):
    off_ref, sink_ref, q_ref, tseg_ref, pad_ref = refs[:5]
    rows_refs = refs[5 : 5 + count]
    rest = refs[5 + count :]
    state_ref = None if first else rest[0]
    out_ref = rest[0 if first else 1]
    q_scr, = rest[(1 if first else 2) :]
    tokens = q_ref.shape[0]
    heads = q_ref.shape[1] // 64
    groups = 2
    slots = (rows_refs[0].shape[0] - 16) // groups
    per = heads // groups
    zero = jnp.zeros((tokens, 64), BF16)
    scale = jnp.array(0.125, BF16)
    for h in range(heads):
        q_scr[h * tokens : (h + 1) * tokens, :] = jnp.concatenate([q_ref[:, h * 64 : h * 64 + 64] * scale, zero], axis=1)
    tseg = to_column(tseg_ref[...].astype(F32))
    tok = iota((tokens, 128), 0).astype(F32)
    biases = []
    for b in range(count):
        meta = rows_refs[b][groups * slots :, :].astype(F32)
        n = slots // 128
        parts = []
        for c in range(n):
            seg, order = meta[c : c + 1, :], meta[n + c : n + c + 1, :]
            seen = (seg == tseg) & ((order < 0.0) | (order + off_ref[b].astype(F32) <= tok))
            parts.append(jnp.where(seen, 0.0, HIDE))
        biases.append(jnp.concatenate(parts, axis=1))
    left = iota((slots, 128), 1) < 64
    lanes = iota((4 * tokens, 128), 1)
    for g in range(groups):
        keys = [rows_refs[b][g * slots : (g + 1) * slots, :] for b in range(count)]
        vals = [jnp.where(left, jnp.ones_like(k), k) for k in keys]
        for part in range(per // 4):
            h0 = g * per + part * 4
            q = q_scr[h0 * tokens : (h0 + 4) * tokens, :]
            scores = []
            for b in range(count):
                s = dot_nt(q, keys[b]).reshape(4, tokens, slots) + biases[b][None]
                scores.append(s.reshape(4 * tokens, slots))
            if first:
                peak = jnp.concatenate([jnp.full((tokens, 1), sink_ref[h0 + i], F32) for i in range(4)], axis=0)
                total = jnp.where(lanes < 64, 1.0, 0.0)
            else:
                state = state_ref[h0 * tokens : (h0 + 4) * tokens, :]
                peak = state[:, 32:33]
                total = state
            top = functools.reduce(jnp.maximum, [jnp.max(s, axis=1, keepdims=True) for s in scores], peak)
            total = total * jnp.exp(peak - top)
            for b in range(count):
                weights = jnp.exp(scores[b] - top).astype(BF16)
                total = total + jnp.dot(weights, vals[b], preferred_element_type=F32)
            if not last:
                out_ref[h0 * tokens : (h0 + 4) * tokens, :] = jnp.where((lanes >= 32) & (lanes < 64), top, total)
            else:
                live = to_column(pad_ref[...].astype(F32))
                for i in range(0, 4, 2):
                    pair = []
                    for u in (i, i + 1):
                        one = total[u * tokens : (u + 1) * tokens, :]
                        pair.append(one[:, 64:128] / one[:, 0:1] * live)
                    out_ref[:, (h0 + i) * 64 : (h0 + i + 2) * 64] = jnp.concatenate(pair, axis=1).astype(BF16)


def attend(first, last, off, sink, q, tseg, pad, rows, state):
    count = len(rows)
    tokens, width = q.shape
    heads = width // 64
    out = jax.ShapeDtypeStruct((tokens, width), BF16) if last else jax.ShapeDtypeStruct((heads * tokens, 128), F32)
    args = [off, sink, q, tseg, pad, *rows] + ([] if first else [state])
    return pl.pallas_call(
        functools.partial(attend_kernel, first, last, count),
        out_shape=out,
        in_specs=[SMEM, SMEM] + [VMEM] * (len(args) - 2),
        out_specs=VMEM,
        scratch_shapes=[pltpu.VMEM((heads * tokens, 128), BF16)],
        compiler_params=pltpu.CompilerParams(vmem_limit_bytes=40 * 2**20),
        cost_estimate=pl.CostEstimate(flops=4 * heads * tokens * 512 * count * 128, bytes_accessed=3 * 2**20, transcendentals=heads * tokens * 512 * count),
    )(*args)


def project_kernel(pos_ref, own_ref, other_ref, w0_ref, w1_ref, w2_ref, w3_ref, keep_a, keep_b, send_a, send_b):
    core, swap = pos_ref[0], pos_ref[1]
    tokens = own_ref.shape[0]
    rows = jnp.concatenate([own_ref[...], other_ref[...]], axis=0)

    def block(one, two):
        a = jnp.dot(rows, one[...], preferred_element_type=F32).astype(BF16)
        b = jnp.dot(rows, two[...], preferred_element_type=F32).astype(BF16)
        return jnp.where(core == 0, jnp.concatenate([a, b], axis=1), jnp.concatenate([b, a], axis=1))

    here, there = block(w0_ref, w1_ref), block(w2_ref, w3_ref)
    a = jnp.where(swap == 0, here, there)
    b = jnp.where(swap == 0, there, here)
    keep_a[...] = a[:tokens]
    send_a[...] = a[tokens:]
    keep_b[...] = b[:tokens]
    send_b[...] = b[tokens:]


def tuned(queries, new_kv, kv_cache, cache_seg, cache_slot, token_seg, pad_mask, sink_logits, out_weight, out_bias):
    tokens, slots = queries.shape[0], kv_cache.shape[0]
    groups = kv_cache.shape[1]
    plane, own = lax.axis_index("gx"), lax.axis_index("gy")
    core, x, y = own % 2, (own // 2) % 2, own // 4

    def gy(value, m):
        return lax.ppermute(value, "gy", [(i, i ^ m) for i in range(8)])

    def gx(value, m):
        return lax.ppermute(value, "gx", [(i, i ^ m) for i in range(4)])

    tseg, pad = token_seg.reshape(1, tokens), pad_mask.reshape(1, tokens)
    cache, rows = pl.pallas_call(
        prep_kernel,
        out_shape=(
            jax.ShapeDtypeStruct((slots, groups * 128), BF16),
            jax.ShapeDtypeStruct((groups * slots + 16, 128), BF16),
        ),
        in_specs=[SMEM] + [VMEM] * 6,
        out_specs=(VMEM, VMEM),
        compiler_params=pltpu.CompilerParams(vmem_limit_bytes=32 * 2**20),
    )(
        (own * slots).reshape(1).astype(jnp.int32),
        kv_cache.reshape(slots, groups * 128),
        new_kv.reshape(tokens, groups * 128),
        cache_seg.reshape(1, slots),
        cache_slot.reshape(1, tokens),
        tseg,
        pad,
    )
    cache_out = cache.reshape(slots, groups, 128)

    rows_x = gy(rows, 2)
    rows_y = gy(rows, 4)
    rows_d = gy(rows_x, 4)
    near = [rows, gy(rows, 1)]
    along_x = [rows_x, gy(rows_x, 1)]
    along_y = [rows_y, gy(rows_y, 1)]
    diagonal = [rows_d, gy(rows_d, 1)]
    w1 = gy(out_weight, 1)
    w2 = gy(out_weight, 2)
    w3 = gy(w2, 1)

    def offsets(m):
        return jnp.stack([((own ^ m) - own) * tokens, ((own ^ m ^ 1) - own) * tokens]).astype(jnp.int32)

    step = functools.partial(attend, sink=sink_logits, q=queries, tseg=tseg, pad=pad)
    state = step(True, False, offsets(0), rows=near, state=None)
    state = step(False, False, offsets(2), rows=along_x, state=state)
    state = step(False, False, offsets(4), rows=along_y, state=state)
    attention = step(False, True, offsets(6), rows=diagonal, state=state)
    other = gy(attention, 4)

    width = out_weight.shape[1] * 2
    part = jax.ShapeDtypeStruct((tokens, width), BF16)
    low = plane % 2
    pos = jnp.stack([core, jnp.where(x == 1 - low, 0, 1)]).astype(jnp.int32)
    keep_a, keep_b, send_a, send_b = pl.pallas_call(
        project_kernel,
        out_shape=(part,) * 4,
        in_specs=[SMEM] + [VMEM] * 6,
        out_specs=(VMEM,) * 4,
        compiler_params=pltpu.CompilerParams(vmem_limit_bytes=32 * 2**20),
    )(pos, attention, other, out_weight, w1, w2, w3)

    got_a = gy(send_a, 4)
    got_z = gx(keep_a, 1)
    got_b = gy(send_b, 4)
    got_w = gx(got_a, 1)
    mine = keep_b.astype(F32) + got_z.astype(F32)
    theirs = got_b.astype(F32) + got_w.astype(F32)
    same = y == plane // 2
    final = jnp.where(same, mine, theirs)
    away = jnp.where(same, theirs, mine).astype(BF16)
    got = gx(away, 2)
    return (final + got.astype(F32) + out_bias).astype(BF16), cache_out


def plain(queries, new_kv, kv_cache, cache_seg, cache_slot, token_seg, pad_mask, sink_logits, out_weight, out_bias):
    local_tokens = queries.shape[0]
    local_slots = kv_cache.shape[0]
    local_groups = kv_cache.shape[1]
    head_dim = kv_cache.shape[2] // 2
    group_heads = queries.shape[1] // (local_groups * head_dim)
    scale = head_dim ** (-0.5)
    own_index = lax.axis_index("gy")
    first_token = own_index * local_tokens
    live_rows = pad_mask == 1
    target = jnp.where(live_rows, cache_slot - own_index * local_slots, local_slots)
    cache_out = kv_cache.at[target].set(new_kv, mode="drop")
    token_index = first_token + jnp.arange(local_tokens, dtype=jnp.int32)
    slot_seg = cache_seg.at[target].set(token_seg, mode="drop")
    slot_order = jnp.full((local_slots,), -1, jnp.int32).at[target].set(token_index, mode="drop")
    sink_table = sink_logits.reshape(local_groups, group_heads)
    query_heads = queries.reshape(local_tokens, local_groups, group_heads, head_dim)
    initial = (
        jnp.broadcast_to(sink_table[:, :, None], (local_groups, group_heads, local_tokens)),
        jnp.ones((local_groups, group_heads, local_tokens), jnp.float32),
        jnp.zeros((local_groups, group_heads, local_tokens, head_dim), jnp.float32),
    )
    kv_rows = lax.all_gather(cache_out, "gy", axis=0, tiled=True)
    seg_rows = lax.all_gather(slot_seg, "gy", axis=0, tiled=True)
    order_rows = lax.all_gather(slot_order, "gy", axis=0, tiled=True)
    total_rows = kv_rows.shape[0]
    blk_rows = math.gcd(total_rows, 512)
    count_blocks = total_rows // blk_rows
    stacked = (
        kv_rows.reshape(count_blocks, blk_rows, local_groups, 2 * head_dim),
        seg_rows.reshape(count_blocks, blk_rows),
        order_rows.reshape(count_blocks, blk_rows),
    )

    def one_block(running, block_data):
        run_peak, weight_sum, weighted = running
        block_kv, block_seg, block_order = block_data
        visible = (block_seg[None, :] == token_seg[:, None]) & (block_order[None, :] <= token_index[:, None])
        scores = (
            jnp.einsum("tgqd,cgd->gqtc", query_heads, block_kv[:, :, :head_dim], preferred_element_type=jnp.float32)
            * scale
        )
        new_peak = jnp.maximum(run_peak, jnp.max(jnp.where(visible, scores, -jnp.inf), axis=-1))
        rescale = jnp.exp(run_peak - new_peak)
        weights = jnp.where(visible, jnp.exp(scores - new_peak[..., None]), 0.0)
        weight_sum = weight_sum * rescale + jnp.sum(weights, axis=-1)
        weighted = weighted * rescale[..., None] + jnp.einsum(
            "gqtc,cgd->gqtd",
            weights.astype(jnp.bfloat16),
            block_kv[:, :, head_dim:],
            preferred_element_type=jnp.float32,
        )
        return ((new_peak, weight_sum, weighted), None)

    result, unused = lax.scan(one_block, initial, stacked)
    run_peak, weight_sum, weighted = result
    attn_heads = jnp.transpose(weighted / weight_sum[..., None], (2, 0, 1, 3)).reshape(
        local_tokens, local_groups * group_heads * head_dim
    )
    attention = (attn_heads * pad_mask[:, None].astype(jnp.float32)).astype(jnp.bfloat16)
    partial_out = jnp.dot(
        attention, lax.all_gather(out_weight, "gy", axis=1, tiled=True), preferred_element_type=jnp.float32
    )
    summed = lax.psum_scatter(
        partial_out.astype(jnp.bfloat16), "gx", scatter_dimension=1, tiled=True
    ).astype(jnp.float32)
    return ((summed + out_bias).astype(jnp.bfloat16), cache_out)


def solution(mesh):
    placed = (
        P("gy", "gx"),
        P("gy", "gx", None),
        P("gy", "gx", None),
        P("gy"),
        P("gy"),
        P("gy"),
        P("gy"),
        P("gx"),
        P("gx", "gy"),
        P("gx"),
    )
    small = mesh.shape["gy"] == 8 and mesh.shape["gx"] == 4
    return jax.shard_map(
        tuned if small else plain,
        mesh=mesh,
        in_specs=placed,
        out_specs=(P("gy", "gx"), P("gy", "gx", None)),
        check_vma=False,
    )
```

```python
import functools
import math

import jax
import jax.numpy as jnp
from jax import lax
from jax.experimental import pallas as pl
from jax.experimental.pallas import tpu as pltpu
from jax.sharding import PartitionSpec as P

F32 = jnp.float32
BF16 = jnp.bfloat16
HIDE = -1e30
VMEM = pl.BlockSpec(memory_space=pltpu.VMEM)
SMEM = pl.BlockSpec(memory_space=pltpu.SMEM)
HBM = pl.BlockSpec(memory_space=pltpu.HBM)


def iota(shape, dim):
    return lax.broadcasted_iota(jnp.int32, shape, dim)


def to_column(row):
    n = row.shape[1]
    eye = iota((n, n), 0) == iota((n, n), 1)
    return jnp.sum(jnp.where(eye, row, 0.0), axis=1, keepdims=True)


def dot_nt(a, b):
    return lax.dot_general(a, b, (((1,), (1,)), ((), ())), preferred_element_type=F32)


def merged(base_ref, kv_ref, new_ref, slot_ref, pad_ref):
    slots, tokens = kv_ref.shape[0], new_ref.shape[0]
    groups = kv_ref.shape[1] // 128
    target = jnp.where(pad_ref[...] == 1, slot_ref[...] - base_ref[0], -1).astype(F32)
    place = (iota((slots, tokens), 0).astype(F32) == target).astype(BF16)
    moved = jnp.dot(place, new_ref[...], preferred_element_type=F32)
    written = jnp.dot(place, jnp.ones((tokens, 128), BF16), preferred_element_type=F32)
    written = jnp.concatenate([written] * groups, axis=1)
    return jnp.where(written > 0.5, moved, kv_ref[...].astype(F32)).astype(BF16), target


def cache_kernel(base_ref, kv_ref, new_ref, slot_ref, pad_ref, cache_ref):
    cache_ref[...] = merged(base_ref, kv_ref, new_ref, slot_ref, pad_ref)[0]


def sort_kernel(base_ref, *refs):
    sources, rows_ref, held, arrived = refs[:6], refs[6], refs[7:13], refs[13]
    copies = [pltpu.make_async_copy(a, b, arrived.at[i]) for i, (a, b) in enumerate(zip(sources, held))]
    for copy in copies:
        copy.start()
    for copy in copies:
        copy.wait()
    kv_ref, new_ref, slot_ref, pad_ref, cseg_ref, tseg_ref = held
    slots, tokens = kv_ref.shape[0], new_ref.shape[0]
    groups = kv_ref.shape[1] // 128
    cache, target = merged(base_ref, kv_ref, new_ref, slot_ref, pad_ref)
    back = to_column(target) == iota((tokens, slots), 1).astype(F32)
    order = jnp.sum(jnp.where(back, (iota((tokens, slots), 0) + 1).astype(F32), 0.0), axis=0, keepdims=True) - 1.0
    new_seg = jnp.sum(jnp.where(back, to_column(tseg_ref[...].astype(F32)), 0.0), axis=0, keepdims=True)
    seg = jnp.where(order >= 0.0, new_seg, cseg_ref[...].astype(F32))
    lane = iota((1, slots), 1).astype(F32)
    key = jnp.where(seg < 0.0, 64.0, seg) * slots + lane
    rank = jnp.sum(jnp.where(to_column(key) < key, 1.0, 0.0), axis=0, keepdims=True)
    perm = (iota((slots, slots), 0).astype(F32) == rank).astype(BF16)
    rows = jnp.dot(perm, cache, preferred_element_type=F32).astype(BF16)
    wide = groups * 128
    lane, turn = iota((128, wide), 1), iota((128, wide), 0)
    lane = lane - (turn // 64) * 128
    turn = turn % 64
    rows_ref[:slots, :] = dot_nt(rows, (lane == turn).astype(BF16)).astype(BF16)
    vals = dot_nt((lane == turn + 64).astype(BF16), rows).astype(BF16)
    for c in range(slots // 128):
        rows_ref[slots + c * 128 : slots + (c + 1) * 128, :] = vals[:, c * 128 : (c + 1) * 128]
    sub = iota((8, slots), 0)
    labels = jnp.where(sub == 0, seg, jnp.where(sub == 1, order, 0.0)).astype(BF16)
    labels = dot_nt(labels, perm)
    parts = [labels[r : r + 1, c : c + 128] for r in range(2) for c in range(0, slots, 128)]
    parts.append(jnp.zeros((16 - len(parts), 128), F32))
    rows_ref[2 * slots :, :] = jnp.concatenate(parts, axis=0).astype(BF16)


def attend_kernel(first, last, count, *refs):
    off_ref, sink_ref, seg_ref, q_ref, tseg_ref, pad_ref = refs[:6]
    rows_refs = refs[6 : 6 + count]
    given_ref, out_ref, extra_ref, q_scr, key_scr, val_scr, bias_scr, acc_scr, moved = refs[6 + count :]
    if first:
        load = pltpu.make_async_copy(given_ref, extra_ref, moved.at[0])
    else:
        load = pltpu.make_async_copy(given_ref, acc_scr, moved.at[0])
        extra_ref[...] = jnp.zeros_like(extra_ref)
    load.start()
    tokens = q_ref.shape[1]
    heads = q_ref.shape[0] // 64
    slots = (rows_refs[0].shape[0] - 16) // 2
    tiles = slots // 128
    zero = jnp.zeros((64, tokens), BF16)
    scale = jnp.array(0.125, BF16)
    for h in range(heads):
        q = q_ref[h * 64 : (h + 1) * 64, :] * scale
        pair = [q, zero] if h < heads // 2 else [zero, q]
        q_scr[:, h * tokens : (h + 1) * tokens] = jnp.concatenate(pair, axis=0)
    tseg = tseg_ref[...].astype(F32)
    tok = iota((128, tokens), 1).astype(F32)
    low, high = seg_ref[0].astype(F32), seg_ref[tokens - 1].astype(F32)

    eye = (iota((128, 128), 0) == iota((128, 128), 1)).astype(BF16)
    row = iota((16, 128), 0)
    labels, flags = [], jnp.zeros((16, 1), F32)
    for b in range(count):
        meta = rows_refs[b][2 * slots :, :]
        labels.append(dot_nt(eye, meta))
        meta = meta.astype(F32)
        hit = jnp.where((meta >= low) & (meta <= high) & (row < tiles), 1.0, 0.0)
        place = jnp.left_shift(1, iota((16, 1), 0) + b * tiles).astype(F32)
        flags = flags + jnp.max(hit, axis=1, keepdims=True) * place
    flags = jnp.sum(flags).astype(jnp.int32)

    used = jnp.int32(0)
    for b in range(count):
        for c in range(tiles):
            wanted = ((flags >> (b * tiles + c)) & 1) == 1

            @pl.when(wanted)
            def _(b=b, c=c, used=used):
                seg, order = labels[b][:, c : c + 1], labels[b][:, tiles + c : tiles + c + 1]
                seen = (seg == tseg) & ((order < 0.0) | (order + off_ref[b].astype(F32) <= tok))
                at = pl.multiple_of(used * 128, 128)
                bias_scr[pl.ds(at, 128), :] = jnp.where(seen, 0.0, HIDE)
                key_scr[pl.ds(at, 128), :] = rows_refs[b][c * 128 : (c + 1) * 128, :]
                val_scr[:, pl.ds(at, 128)] = rows_refs[b][slots + c * 128 : slots + (c + 1) * 128, :]

            used = used + wanted.astype(jnp.int32)
    for extra in range(1):
        at = pl.multiple_of(used * 128, 128)
        bias_scr[pl.ds(at, 128), :] = jnp.full((128, tokens), HIDE, F32)
        key_scr[pl.ds(at, 128), :] = jnp.zeros((128, 128), BF16)
        val_scr[:, pl.ds(at, 128)] = jnp.zeros((128, 128), BF16)

    if first:
        for h in range(heads):
            span = slice(h * tokens, (h + 1) * tokens)
            acc_scr[:64, span] = jnp.zeros((64, tokens), F32)
            acc_scr[64:72, span] = jnp.ones((8, tokens), F32)
            acc_scr[72:80, span] = jnp.full((8, tokens), sink_ref[h], F32)
    else:
        load.wait()
    half = heads // 2 * tokens

    def pair(index, carry):
        at = pl.multiple_of(index * 256, 256)
        keys = key_scr[pl.ds(at, 256), :]
        bias = jnp.concatenate([bias_scr[pl.ds(at, 256), :]] * (heads // 2), axis=1)
        ones = jnp.ones((16, 256), BF16)
        spans = [slice(group * half, (group + 1) * half) for group in range(2)]
        scores = [jnp.dot(keys, q_scr[:, span], preferred_element_type=F32) + bias for span in spans]
        peaks = [acc_scr[72:73, span] for span in spans]
        tops = [jnp.maximum(jnp.max(s, axis=0, keepdims=True), p) for s, p in zip(scores, peaks)]
        weights = [jnp.exp(s - t).astype(BF16) for s, t in zip(scores, tops)]
        for group, span in enumerate(spans):
            vals = jnp.concatenate([val_scr[group * 64 : (group + 1) * 64, pl.ds(at, 256)], ones], axis=0)
            new = jnp.dot(vals, weights[group], preferred_element_type=F32)[:72, :]
            acc_scr[:72, span] = acc_scr[:72, span] * jnp.exp(peaks[group] - tops[group]) + new
            acc_scr[72:80, span] = jnp.broadcast_to(tops[group], (8, half))
        return carry

    lax.fori_loop(0, (used + 1) // 2, pair, 0)
    if not last:
        save = pltpu.make_async_copy(acc_scr, out_ref, moved.at[1])
        save.start()
        save.wait()
        if first:
            load.wait()
    else:
        live = pad_ref[...].astype(F32)
        for h in range(heads):
            span = slice(h * tokens, (h + 1) * tokens)
            out_ref[h * 64 : (h + 1) * 64, :] = (acc_scr[:64, span] / acc_scr[64:65, span] * live).astype(BF16)


def attend(first, last, off, sink, q, seg, tseg, pad, rows, given):
    count = len(rows)
    width, tokens = q.shape
    heads = width // 64
    slots = (rows[0].shape[0] - 16) // 2
    out = jax.ShapeDtypeStruct((width, tokens), BF16) if last else jax.ShapeDtypeStruct((80, heads * tokens), F32)
    args = [off, sink, seg, q, tseg, pad, *rows, given]
    extra = jax.ShapeDtypeStruct(given.shape, given.dtype) if first else jax.ShapeDtypeStruct((8, 128), F32)
    return pl.pallas_call(
        functools.partial(attend_kernel, first, last, count),
        out_shape=(out, extra),
        in_specs=[SMEM] * 3 + [VMEM] * (3 + count) + [HBM],
        out_specs=(VMEM if last else HBM, HBM if first else VMEM),
        scratch_shapes=[
            pltpu.VMEM((128, heads * tokens), BF16),
            pltpu.VMEM((count * slots + 256, 128), BF16),
            pltpu.VMEM((128, count * slots + 256), BF16),
            pltpu.VMEM((count * slots + 256, tokens), F32),
            pltpu.VMEM((80, heads * tokens), F32),
            pltpu.SemaphoreType.DMA((2,)),
        ],
        compiler_params=pltpu.CompilerParams(vmem_limit_bytes=16 * 2**20),
        cost_estimate=pl.CostEstimate(
            flops=4 * heads * tokens * slots * count * 128,
            bytes_accessed=3 * 2**20,
            transcendentals=heads * tokens * slots * count,
        ),
    )(*args)


def project_kernel(pos_ref, rows_ref, w0_ref, w1_ref, w2_ref, w3_ref, a_ref, b_ref):
    core, swap = pos_ref[0], pos_ref[1]
    rows = rows_ref[...]

    def block(one, two):
        a = jnp.dot(one[...], rows, preferred_element_type=F32)
        b = jnp.dot(two[...], rows, preferred_element_type=F32)
        return jnp.where(core == 0, jnp.concatenate([a, b], axis=0), jnp.concatenate([b, a], axis=0)).astype(BF16)

    here, there = block(w0_ref, w1_ref), block(w2_ref, w3_ref)
    a_ref[...] = jnp.where(swap == 0, here, there)
    b_ref[...] = jnp.where(swap == 0, there, here)


def tuned(queries, new_kv, kv_cache, cache_seg, cache_slot, token_seg, pad_mask, sink_logits, out_weight, out_bias):
    tokens, slots = queries.shape[0], kv_cache.shape[0]
    groups = kv_cache.shape[1]
    plane, own = lax.axis_index("gx"), lax.axis_index("gy")
    core, x, y = own % 2, (own // 2) % 2, own // 4

    def gy(value, m):
        return lax.ppermute(value, "gy", [(i, i ^ m) for i in range(8)])

    def gx(value, m):
        return lax.ppermute(value, "gx", [(i, i ^ m) for i in range(4)])

    tseg, pad = token_seg.reshape(1, tokens), pad_mask.reshape(1, tokens)
    store = [
        (own * slots).reshape(1).astype(jnp.int32),
        kv_cache.reshape(slots, groups * 128),
        new_kv.reshape(tokens, groups * 128),
        cache_slot.reshape(1, tokens),
        pad,
    ]
    rows = pl.pallas_call(
        sort_kernel,
        out_shape=jax.ShapeDtypeStruct((groups * slots + 16, 128), BF16),
        in_specs=[SMEM] + [HBM] * 6,
        out_specs=VMEM,
        scratch_shapes=[
            pltpu.VMEM((slots, groups * 128), BF16),
            pltpu.VMEM((tokens, groups * 128), BF16),
            pltpu.VMEM((1, tokens), jnp.int32),
            pltpu.VMEM((1, tokens), jnp.int32),
            pltpu.VMEM((1, slots), jnp.int32),
            pltpu.VMEM((1, tokens), jnp.int32),
            pltpu.SemaphoreType.DMA((6,)),
        ],
        compiler_params=pltpu.CompilerParams(vmem_limit_bytes=16 * 2**20),
    )(*store, cache_seg.reshape(1, slots), tseg)

    rows_x = gy(rows, 2)
    rows_y = gy(rows, 4)
    near = [rows, gy(rows, 1)]
    w0 = out_weight.T

    def offsets(m):
        return jnp.stack([((own ^ m) - own) * tokens, ((own ^ m ^ 1) - own) * tokens]).astype(jnp.int32)

    turned = queries.T
    step = functools.partial(attend, sink=sink_logits, q=turned, seg=token_seg, tseg=tseg, pad=pad)
    state, sent = step(True, False, offsets(0), rows=near, given=w0)
    rows_d = gy(rows_x, 4)
    w2 = gy(sent, 2)
    along = [rows_x, gy(rows_x, 1), rows_y, gy(rows_y, 1)]
    both = jnp.concatenate([offsets(2), offsets(4)])
    state, done = step(False, False, both, rows=along, given=state)
    w1 = gy(sent, 1)
    diagonal = [rows_d, gy(rows_d, 1)]
    attention, done = step(False, True, offsets(6), rows=diagonal, given=state)
    other = gy(attention, 4)
    w2 = w2 + done[0, 0].astype(BF16)
    w3 = gy(w2, 1)

    part = jax.ShapeDtypeStruct((out_weight.shape[1] * 2, tokens), BF16)
    pos = jnp.stack([core, jnp.where(x == 1 - plane % 2, 0, 1)]).astype(jnp.int32)
    project = pl.pallas_call(
        project_kernel,
        out_shape=(part, part),
        in_specs=[SMEM] + [VMEM] * 5,
        out_specs=(VMEM, VMEM),
        compiler_params=pltpu.CompilerParams(vmem_limit_bytes=16 * 2**20),
        cost_estimate=pl.CostEstimate(flops=2 * 1024 * 1440 * 256, bytes_accessed=4 * 2**20, transcendentals=0),
    )
    keep_a, keep_b = project(pos, attention, w0, w1, w2, w3)
    got_k = gx(keep_a, 1)
    send_a, send_b = project(pos, other, w0, w1, w2, w3)
    got_s = gx(send_a, 1)
    got = gy((send_b.astype(F32) + got_s.astype(F32)).astype(BF16), 4)
    cache = pl.pallas_call(
        cache_kernel,
        out_shape=jax.ShapeDtypeStruct((slots, groups * 128), BF16),
        in_specs=[SMEM] + [VMEM] * 4,
        out_specs=VMEM,
        compiler_params=pltpu.CompilerParams(vmem_limit_bytes=16 * 2**20),
    )(*store)
    mine = keep_b.astype(F32) + got_k.astype(F32)
    theirs = got.astype(F32)
    same = y == plane // 2
    final = jnp.where(same, mine, theirs)
    away = jnp.where(same, theirs, mine).astype(BF16)
    last = gx(away, 2)
    out = (final + last.astype(F32) + out_bias[:, None]).astype(BF16)
    return out.T, cache.reshape(slots, groups, 128)


def plain(queries, new_kv, kv_cache, cache_seg, cache_slot, token_seg, pad_mask, sink_logits, out_weight, out_bias):
    local_tokens = queries.shape[0]
    local_slots = kv_cache.shape[0]
    local_groups = kv_cache.shape[1]
    head_dim = kv_cache.shape[2] // 2
    group_heads = queries.shape[1] // (local_groups * head_dim)
    scale = head_dim ** (-0.5)
    own_index = lax.axis_index("gy")
    first_token = own_index * local_tokens
    live_rows = pad_mask == 1
    target = jnp.where(live_rows, cache_slot - own_index * local_slots, local_slots)
    cache_out = kv_cache.at[target].set(new_kv, mode="drop")
    token_index = first_token + jnp.arange(local_tokens, dtype=jnp.int32)
    slot_seg = cache_seg.at[target].set(token_seg, mode="drop")
    slot_order = jnp.full((local_slots,), -1, jnp.int32).at[target].set(token_index, mode="drop")
    sink_table = sink_logits.reshape(local_groups, group_heads)
    query_heads = queries.reshape(local_tokens, local_groups, group_heads, head_dim)
    initial = (
        jnp.broadcast_to(sink_table[:, :, None], (local_groups, group_heads, local_tokens)),
        jnp.ones((local_groups, group_heads, local_tokens), jnp.float32),
        jnp.zeros((local_groups, group_heads, local_tokens, head_dim), jnp.float32),
    )
    kv_rows = lax.all_gather(cache_out, "gy", axis=0, tiled=True)
    seg_rows = lax.all_gather(slot_seg, "gy", axis=0, tiled=True)
    order_rows = lax.all_gather(slot_order, "gy", axis=0, tiled=True)
    total_rows = kv_rows.shape[0]
    blk_rows = math.gcd(total_rows, 512)
    count_blocks = total_rows // blk_rows
    stacked = (
        kv_rows.reshape(count_blocks, blk_rows, local_groups, 2 * head_dim),
        seg_rows.reshape(count_blocks, blk_rows),
        order_rows.reshape(count_blocks, blk_rows),
    )

    def one_block(running, block_data):
        run_peak, weight_sum, weighted = running
        block_kv, block_seg, block_order = block_data
        visible = (block_seg[None, :] == token_seg[:, None]) & (block_order[None, :] <= token_index[:, None])
        scores = (
            jnp.einsum("tgqd,cgd->gqtc", query_heads, block_kv[:, :, :head_dim], preferred_element_type=jnp.float32)
            * scale
        )
        new_peak = jnp.maximum(run_peak, jnp.max(jnp.where(visible, scores, -jnp.inf), axis=-1))
        rescale = jnp.exp(run_peak - new_peak)
        weights = jnp.where(visible, jnp.exp(scores - new_peak[..., None]), 0.0)
        weight_sum = weight_sum * rescale + jnp.sum(weights, axis=-1)
        weighted = weighted * rescale[..., None] + jnp.einsum(
            "gqtc,cgd->gqtd",
            weights.astype(jnp.bfloat16),
            block_kv[:, :, head_dim:],
            preferred_element_type=jnp.float32,
        )
        return ((new_peak, weight_sum, weighted), None)

    result, unused = lax.scan(one_block, initial, stacked)
    run_peak, weight_sum, weighted = result
    attn_heads = jnp.transpose(weighted / weight_sum[..., None], (2, 0, 1, 3)).reshape(
        local_tokens, local_groups * group_heads * head_dim
    )
    attention = (attn_heads * pad_mask[:, None].astype(jnp.float32)).astype(jnp.bfloat16)
    partial_out = jnp.dot(
        attention, lax.all_gather(out_weight, "gy", axis=1, tiled=True), preferred_element_type=jnp.float32
    )
    summed = lax.psum_scatter(
        partial_out.astype(jnp.bfloat16), "gx", scatter_dimension=1, tiled=True
    ).astype(jnp.float32)
    return ((summed + out_bias).astype(jnp.bfloat16), cache_out)


def solution(mesh):
    placed = (
        P("gy", "gx"),
        P("gy", "gx", None),
        P("gy", "gx", None),
        P("gy"),
        P("gy"),
        P("gy"),
        P("gy"),
        P("gx"),
        P("gx", "gy"),
        P("gx"),
    )
    small = mesh.shape["gy"] == 8 and mesh.shape["gx"] == 4
    return jax.shard_map(
        tuned if small else plain,
        mesh=mesh,
        in_specs=placed,
        out_specs=(P("gy", "gx"), P("gy", "gx", None)),
        check_vma=False,
    )
```

```python
import functools
import math

import jax
import jax.numpy as jnp
from jax import lax
from jax.experimental import pallas as pl
from jax.experimental.pallas import tpu as pltpu
from jax.sharding import PartitionSpec as P

F32 = jnp.float32
BF16 = jnp.bfloat16
HIDE = -1e30
VMEM = pl.BlockSpec(memory_space=pltpu.VMEM)
SMEM = pl.BlockSpec(memory_space=pltpu.SMEM)
HBM = pl.BlockSpec(memory_space=pltpu.HBM)


def iota(shape, dim):
    return lax.broadcasted_iota(jnp.int32, shape, dim)


def to_column(row):
    n = row.shape[1]
    eye = iota((n, n), 0) == iota((n, n), 1)
    return jnp.sum(jnp.where(eye, row, 0.0), axis=1, keepdims=True)


def dot_nt(a, b):
    return lax.dot_general(a, b, (((1,), (1,)), ((), ())), preferred_element_type=F32)


def merged(base_ref, kv_ref, new_ref, slot_ref, pad_ref):
    slots, tokens = kv_ref.shape[0], new_ref.shape[0]
    groups = kv_ref.shape[1] // 128
    target = jnp.where(pad_ref[...] == 1, slot_ref[...] - base_ref[0], -1).astype(F32)
    place = (iota((slots, tokens), 0).astype(F32) == target).astype(BF16)
    moved = jnp.dot(place, new_ref[...], preferred_element_type=F32)
    written = jnp.dot(place, jnp.ones((tokens, 128), BF16), preferred_element_type=F32)
    written = jnp.concatenate([written] * groups, axis=1)
    return jnp.where(written > 0.5, moved, kv_ref[...].astype(F32)).astype(BF16), target


def cache_kernel(base_ref, kv_ref, new_ref, slot_ref, pad_ref, cache_ref):
    cache_ref[...] = merged(base_ref, kv_ref, new_ref, slot_ref, pad_ref)[0]


def sort_kernel(base_ref, *refs):
    sources, rows_ref, held, arrived = refs[:6], refs[6], refs[7:13], refs[13]
    copies = [pltpu.make_async_copy(a, b, arrived.at[i]) for i, (a, b) in enumerate(zip(sources, held))]
    for copy in copies:
        copy.start()
    for copy in copies:
        copy.wait()
    kv_ref, new_ref, slot_ref, pad_ref, cseg_ref, tseg_ref = held
    slots, tokens = kv_ref.shape[0], new_ref.shape[0]
    groups = kv_ref.shape[1] // 128
    cache, target = merged(base_ref, kv_ref, new_ref, slot_ref, pad_ref)
    back = to_column(target) == iota((tokens, slots), 1).astype(F32)
    order = jnp.sum(jnp.where(back, (iota((tokens, slots), 0) + 1).astype(F32), 0.0), axis=0, keepdims=True) - 1.0
    new_seg = jnp.sum(jnp.where(back, to_column(tseg_ref[...].astype(F32)), 0.0), axis=0, keepdims=True)
    seg = jnp.where(order >= 0.0, new_seg, cseg_ref[...].astype(F32))
    lane = iota((1, slots), 1).astype(F32)
    key = jnp.where(seg < 0.0, 64.0, seg) * slots + lane
    rank = jnp.sum(jnp.where(to_column(key) < key, 1.0, 0.0), axis=0, keepdims=True)
    perm = (iota((slots, slots), 0).astype(F32) == rank).astype(BF16)
    rows = jnp.dot(perm, cache, preferred_element_type=F32).astype(BF16)
    wide = groups * 128
    lane, turn = iota((128, wide), 1), iota((128, wide), 0)
    lane = lane - (turn // 64) * 128
    turn = turn % 64
    rows_ref[:slots, :] = dot_nt(rows, (lane == turn).astype(BF16)).astype(BF16)
    rows_ref[slots : 2 * slots, :] = dot_nt(rows, (lane == turn + 64).astype(BF16)).astype(BF16)
    sub = iota((8, slots), 0)
    labels = jnp.where(sub == 0, seg, jnp.where(sub == 1, order, 0.0)).astype(BF16)
    labels = dot_nt(labels, perm)
    parts = [labels[r : r + 1, c : c + 128] for r in range(2) for c in range(0, slots, 128)]
    parts.append(jnp.zeros((16 - len(parts), 128), F32))
    rows_ref[2 * slots :, :] = jnp.concatenate(parts, axis=0).astype(BF16)


def attend_kernel(first, last, count, *refs):
    off_ref, sink_ref, seg_ref, q_ref, tseg_ref, pad_ref = refs[:6]
    rows_refs = refs[6 : 6 + count]
    given_ref, out_ref, extra_ref, *sent_ref = refs[6 + count :][: 4 if first else 3]
    q_scr, key_scr, val_scr, label_scr, row_scr, acc_scr, moved = refs[6 + count :][4 if first else 3 :]
    if first:
        load = pltpu.make_async_copy(given_ref, sent_ref[0], moved.at[0])
    else:
        load = pltpu.make_async_copy(given_ref, acc_scr, moved.at[0])
    load.start()
    extra_ref[...] = jnp.zeros_like(extra_ref)
    tokens = q_ref.shape[1]
    heads = q_ref.shape[0] // 64
    slots = (rows_refs[0].shape[0] - 16) // 2
    tiles = slots // 128
    zero = jnp.zeros((64, tokens), BF16)
    scale = jnp.array(0.125, BF16)
    for h in range(heads):
        q = q_ref[h * 64 : (h + 1) * 64, :] * scale
        pair = [q, zero] if h < heads // 2 else [zero, q]
        q_scr[:, h * tokens : (h + 1) * tokens] = jnp.concatenate(pair, axis=0)
    tseg = tseg_ref[...].astype(F32)
    tok = iota((1, tokens), 1).astype(F32)
    low, high = seg_ref[0].astype(F32), seg_ref[tokens - 1].astype(F32)
    eye = (iota((128, 128), 0) == iota((128, 128), 1)).astype(BF16)
    stretches = []
    for b in range(count):
        meta = rows_refs[b][2 * slots :, :].astype(F32)
        real = (iota((16, 128), 0) < tiles) & (meta >= 0.0)
        counts = jnp.where(real & (meta < low), 1.0, 0.0) + jnp.where(real & (meta <= high), 1024.0, 0.0)
        counts = jnp.sum(jnp.sum(counts, axis=0, keepdims=True), axis=1, keepdims=True).astype(jnp.int32)
        begin, end = (counts & 1023) >> 4, (counts >> 10) + 31 >> 4
        stretches.append(begin + (end << 6))
        for c in range(tiles):
            order = meta[tiles + c : tiles + c + 1, :]
            order = jnp.where(order < 0.0, -1.0, jnp.clip(order + off_ref[b].astype(F32), -1.0, tokens))
            label = jnp.concatenate([meta[c : c + 1, :], order, jnp.zeros((14, 128), F32)], axis=0)
            label_scr[b, c * 128 : (c + 1) * 128, :16] = dot_nt(eye, label.astype(BF16))
        label_scr[b, slots:, :16] = jnp.full((32, 16), -1.0, F32)
    packed = [stretches[b] + (stretches[b + 1] << 12) for b in range(0, count, 2)]
    packed = [jnp.sum(p) for p in packed]

    used = jnp.int32(0)
    for b in range(count):
        stretch = packed[b // 2] >> (12 * (b % 2))
        begin = stretch & 63
        steps = jnp.maximum(((stretch >> 6) & 63) - begin, 0) >> 1

        def move(i, carry, b=b, begin=begin, used=used):
            at = pl.multiple_of(begin * 16 + i * 32, 16)
            to = pl.multiple_of(used + i * 32, 32)
            key_scr[pl.ds(to, 32), :] = rows_refs[b][pl.ds(at, 32), :]
            val_scr[pl.ds(to, 32), :] = rows_refs[b][pl.ds(pl.multiple_of(slots + at, 16), 32), :]
            row_scr[pl.ds(to, 32), :] = label_scr[b, pl.ds(at, 32), :]
            return carry

        lax.fori_loop(0, steps, move, 0)
        used = used + steps * 32
    rest = pl.ds(pl.multiple_of(used, 32), 256)
    key_scr[rest, :] = jnp.zeros((256, 128), BF16)
    val_scr[rest, :] = jnp.zeros((256, 128), BF16)
    row_scr[rest, :] = jnp.full((256, 128), -1.0, F32)
    if first:
        for h in range(heads):
            span = slice(h * tokens, (h + 1) * tokens)
            acc_scr[:64, span] = jnp.zeros((64, tokens), F32)
            acc_scr[64:72, span] = jnp.ones((8, tokens), F32)
            acc_scr[72:80, span] = jnp.full((8, tokens), sink_ref[h], F32)
    else:
        load.wait()
    half = heads // 2 * tokens

    def pair(index, carry):
        at = pl.multiple_of(index * 256, 256)
        keys = key_scr[pl.ds(at, 256), :]
        rows = row_scr[pl.ds(at, 256), :]
        seen = (rows[:, :1] == tseg) & (rows[:, 1:2] <= tok)
        bias = jnp.concatenate([jnp.where(seen, 0.0, HIDE)] * (heads // 2), axis=1)
        turned = dot_nt(eye, val_scr[pl.ds(at, 256), :]).astype(BF16)
        ones = jnp.ones((16, 256), BF16)
        spans = [slice(group * half, (group + 1) * half) for group in range(2)]
        scores = [jnp.dot(keys, q_scr[:, span], preferred_element_type=F32) + bias for span in spans]
        peaks = [acc_scr[72:73, span] for span in spans]
        tops = [jnp.maximum(jnp.max(s, axis=0, keepdims=True), p) for s, p in zip(scores, peaks)]
        weights = [jnp.exp(s - t).astype(BF16) for s, t in zip(scores, tops)]
        for group, span in enumerate(spans):
            vals = jnp.concatenate([turned[group * 64 : (group + 1) * 64, :], ones], axis=0)
            new = jnp.dot(vals, weights[group], preferred_element_type=F32)[:72, :]
            acc_scr[:72, span] = acc_scr[:72, span] * jnp.exp(peaks[group] - tops[group]) + new
            acc_scr[72:80, span] = jnp.broadcast_to(tops[group], (8, half))
        return carry

    lax.fori_loop(0, (used + 255) // 256, pair, 0)
    if not last:
        save = pltpu.make_async_copy(acc_scr, out_ref, moved.at[1])
        save.start()
        save.wait()
        if first:
            load.wait()
    else:
        live = pad_ref[...].astype(F32)
        for h in range(heads):
            span = slice(h * tokens, (h + 1) * tokens)
            out_ref[h * 64 : (h + 1) * 64, :] = (acc_scr[:64, span] / acc_scr[64:65, span] * live).astype(BF16)


def attend(first, last, off, sink, q, seg, tseg, pad, rows, given):
    count = len(rows)
    width, tokens = q.shape
    heads = width // 64
    slots = (rows[0].shape[0] - 16) // 2
    if last:
        out = (jax.ShapeDtypeStruct((width, tokens), BF16), jax.ShapeDtypeStruct((1, width), BF16))
    else:
        out = (jax.ShapeDtypeStruct((80, heads * tokens), F32), jax.ShapeDtypeStruct((1, 128), BF16))
    if first:
        out += (jax.ShapeDtypeStruct(given.shape, given.dtype),)
    args = [off, sink, seg, q, tseg, pad, *rows, given]
    return pl.pallas_call(
        functools.partial(attend_kernel, first, last, count),
        out_shape=out,
        in_specs=[SMEM] * 3 + [VMEM] * (3 + count) + [HBM],
        out_specs=(VMEM if last else HBM, VMEM) + ((HBM,) if first else ()),
        scratch_shapes=[
            pltpu.VMEM((128, heads * tokens), BF16),
            pltpu.VMEM((count * slots + 256, 128), BF16),
            pltpu.VMEM((count * slots + 256, 128), BF16),
            pltpu.VMEM((count, slots + 32, 128), F32),
            pltpu.VMEM((count * slots + 256, 128), F32),
            pltpu.VMEM((80, heads * tokens), F32),
            pltpu.SemaphoreType.DMA((2,)),
        ],
        compiler_params=pltpu.CompilerParams(vmem_limit_bytes=16 * 2**20),
        cost_estimate=pl.CostEstimate(
            flops=1 * heads * tokens * slots * count * 128,
            bytes_accessed=10**6,
            transcendentals=0,
        ),
    )(*args)


def project_kernel(pos_ref, rows_ref, w0_ref, w1_ref, w2_ref, *refs):
    core, swap = pos_ref[0], pos_ref[1]
    *w3_refs, a_ref, b_ref = refs
    rows = rows_ref[...]

    def block(one, two):
        a = [jnp.dot(one[...], rows, preferred_element_type=F32)]
        b = [jnp.dot(w[...], rows, preferred_element_type=F32) for w in two]
        return jnp.where(core == 0, jnp.concatenate(a + b, axis=0), jnp.concatenate(b + a, axis=0)).astype(BF16)

    here, there = block(w0_ref, [w1_ref]), block(w2_ref, w3_refs)
    a_ref[...] = jnp.where(swap == 0, here, there)
    b_ref[...] = jnp.where(swap == 0, there, here)


def tuned(queries, new_kv, kv_cache, cache_seg, cache_slot, token_seg, pad_mask, sink_logits, out_weight, out_bias):
    tokens, slots = queries.shape[0], kv_cache.shape[0]
    groups = kv_cache.shape[1]
    plane, own = lax.axis_index("gx"), lax.axis_index("gy")
    core, x, y = own % 2, (own // 2) % 2, own // 4

    def gy(value, m):
        return lax.ppermute(value, "gy", [(i, i ^ m) for i in range(8)])

    def gx(value, m):
        return lax.ppermute(value, "gx", [(i, i ^ m) for i in range(4)])

    tseg, pad = token_seg.reshape(1, tokens), pad_mask.reshape(1, tokens)
    store = [
        (own * slots).reshape(1).astype(jnp.int32),
        kv_cache.reshape(slots, groups * 128),
        new_kv.reshape(tokens, groups * 128),
        cache_slot.reshape(1, tokens),
        pad,
    ]
    rows = pl.pallas_call(
        sort_kernel,
        out_shape=jax.ShapeDtypeStruct((groups * slots + 16, 128), BF16),
        in_specs=[SMEM] + [HBM] * 6,
        out_specs=VMEM,
        scratch_shapes=[
            pltpu.VMEM((slots, groups * 128), BF16),
            pltpu.VMEM((tokens, groups * 128), BF16),
            pltpu.VMEM((1, tokens), jnp.int32),
            pltpu.VMEM((1, tokens), jnp.int32),
            pltpu.VMEM((1, slots), jnp.int32),
            pltpu.VMEM((1, tokens), jnp.int32),
            pltpu.SemaphoreType.DMA((6,)),
        ],
        compiler_params=pltpu.CompilerParams(vmem_limit_bytes=16 * 2**20),
    )(*store, cache_seg.reshape(1, slots), tseg)

    rows_x = gy(rows, 2)
    rows_y = gy(rows, 4)
    near = [rows, gy(rows, 1)]
    w0 = out_weight.T

    def offsets(m):
        return jnp.stack([((own ^ m) - own) * tokens, ((own ^ m ^ 1) - own) * tokens]).astype(jnp.int32)

    turned = queries.T
    step = functools.partial(attend, sink=sink_logits, q=turned, seg=token_seg, tseg=tseg, pad=pad)
    state, zeros, sent = step(True, False, offsets(0), rows=near, given=w0)
    rows_x = rows_x + zeros
    rows_d = gy(rows_x, 4)
    w2 = gy(sent, 2)
    along = [rows_x, gy(rows_x, 1), rows_y, gy(rows_y, 1)]
    both = jnp.concatenate([offsets(2), offsets(4)])
    state, zeros = step(False, False, both, rows=along, given=state)
    w1 = gy(sent, 1)
    rows_d = rows_d + zeros
    diagonal = [rows_d, gy(rows_d, 1)]
    attention, zeros = step(False, True, offsets(6), rows=diagonal, given=state)
    other = gy(attention, 4)
    third = w2.shape[0] // 3
    w3 = [gy(w2[i * third : (i + 1) * third] + zeros, 1) for i in range(3)]

    part = jax.ShapeDtypeStruct((out_weight.shape[1] * 2, tokens), BF16)
    pos = jnp.stack([core, jnp.where(x == 1 - plane % 2, 0, 1)]).astype(jnp.int32)
    project = pl.pallas_call(
        project_kernel,
        out_shape=(part, part),
        in_specs=[SMEM] + [VMEM] * 7,
        out_specs=(VMEM, VMEM),
        compiler_params=pltpu.CompilerParams(vmem_limit_bytes=16 * 2**20),
        cost_estimate=pl.CostEstimate(flops=2 * 1024 * 1440 * 256, bytes_accessed=4 * 2**20, transcendentals=0),
    )
    keep_a, keep_b = project(pos, attention, w0, w1, w2, *w3)
    got_k = gx(keep_a, 1)
    send_a, send_b = project(pos, other, w0, w1, w2, *w3)
    got_s = gx(send_a, 1)
    got = gy((send_b.astype(F32) + got_s.astype(F32)).astype(BF16), 4)
    cache = pl.pallas_call(
        cache_kernel,
        out_shape=jax.ShapeDtypeStruct((slots, groups * 128), BF16),
        in_specs=[SMEM] + [VMEM] * 4,
        out_specs=VMEM,
        compiler_params=pltpu.CompilerParams(vmem_limit_bytes=16 * 2**20),
    )(*store)
    mine = keep_b.astype(F32) + got_k.astype(F32)
    theirs = got.astype(F32)
    same = y == plane // 2
    final = jnp.where(same, mine, theirs)
    away = jnp.where(same, theirs, mine).astype(BF16)
    last = gx(away, 2)
    out = (final + last.astype(F32) + out_bias[:, None]).astype(BF16)
    return out.T, cache.reshape(slots, groups, 128)


def plain(queries, new_kv, kv_cache, cache_seg, cache_slot, token_seg, pad_mask, sink_logits, out_weight, out_bias):
    local_tokens = queries.shape[0]
    local_slots = kv_cache.shape[0]
    local_groups = kv_cache.shape[1]
    head_dim = kv_cache.shape[2] // 2
    group_heads = queries.shape[1] // (local_groups * head_dim)
    scale = head_dim ** (-0.5)
    own_index = lax.axis_index("gy")
    first_token = own_index * local_tokens
    live_rows = pad_mask == 1
    target = jnp.where(live_rows, cache_slot - own_index * local_slots, local_slots)
    cache_out = kv_cache.at[target].set(new_kv, mode="drop")
    token_index = first_token + jnp.arange(local_tokens, dtype=jnp.int32)
    slot_seg = cache_seg.at[target].set(token_seg, mode="drop")
    slot_order = jnp.full((local_slots,), -1, jnp.int32).at[target].set(token_index, mode="drop")
    sink_table = sink_logits.reshape(local_groups, group_heads)
    query_heads = queries.reshape(local_tokens, local_groups, group_heads, head_dim)
    initial = (
        jnp.broadcast_to(sink_table[:, :, None], (local_groups, group_heads, local_tokens)),
        jnp.ones((local_groups, group_heads, local_tokens), jnp.float32),
        jnp.zeros((local_groups, group_heads, local_tokens, head_dim), jnp.float32),
    )
    kv_rows = lax.all_gather(cache_out, "gy", axis=0, tiled=True)
    seg_rows = lax.all_gather(slot_seg, "gy", axis=0, tiled=True)
    order_rows = lax.all_gather(slot_order, "gy", axis=0, tiled=True)
    total_rows = kv_rows.shape[0]
    blk_rows = math.gcd(total_rows, 512)
    count_blocks = total_rows // blk_rows
    stacked = (
        kv_rows.reshape(count_blocks, blk_rows, local_groups, 2 * head_dim),
        seg_rows.reshape(count_blocks, blk_rows),
        order_rows.reshape(count_blocks, blk_rows),
    )

    def one_block(running, block_data):
        run_peak, weight_sum, weighted = running
        block_kv, block_seg, block_order = block_data
        visible = (block_seg[None, :] == token_seg[:, None]) & (block_order[None, :] <= token_index[:, None])
        scores = (
            jnp.einsum("tgqd,cgd->gqtc", query_heads, block_kv[:, :, :head_dim], preferred_element_type=jnp.float32)
            * scale
        )
        new_peak = jnp.maximum(run_peak, jnp.max(jnp.where(visible, scores, -jnp.inf), axis=-1))
        rescale = jnp.exp(run_peak - new_peak)
        weights = jnp.where(visible, jnp.exp(scores - new_peak[..., None]), 0.0)
        weight_sum = weight_sum * rescale + jnp.sum(weights, axis=-1)
        weighted = weighted * rescale[..., None] + jnp.einsum(
            "gqtc,cgd->gqtd",
            weights.astype(jnp.bfloat16),
            block_kv[:, :, head_dim:],
            preferred_element_type=jnp.float32,
        )
        return ((new_peak, weight_sum, weighted), None)

    result, unused = lax.scan(one_block, initial, stacked)
    run_peak, weight_sum, weighted = result
    attn_heads = jnp.transpose(weighted / weight_sum[..., None], (2, 0, 1, 3)).reshape(
        local_tokens, local_groups * group_heads * head_dim
    )
    attention = (attn_heads * pad_mask[:, None].astype(jnp.float32)).astype(jnp.bfloat16)
    partial_out = jnp.dot(
        attention, lax.all_gather(out_weight, "gy", axis=1, tiled=True), preferred_element_type=jnp.float32
    )
    summed = lax.psum_scatter(
        partial_out.astype(jnp.bfloat16), "gx", scatter_dimension=1, tiled=True
    ).astype(jnp.float32)
    return ((summed + out_bias).astype(jnp.bfloat16), cache_out)


def solution(mesh):
    placed = (
        P("gy", "gx"),
        P("gy", "gx", None),
        P("gy", "gx", None),
        P("gy"),
        P("gy"),
        P("gy"),
        P("gy"),
        P("gx"),
        P("gx", "gy"),
        P("gx"),
    )
    small = mesh.shape["gy"] == 8 and mesh.shape["gx"] == 4
    return jax.shard_map(
        tuned if small else plain,
        mesh=mesh,
        in_specs=placed,
        out_specs=(P("gy", "gx"), P("gy", "gx", None)),
        check_vma=False,
    )
```

```python
import functools
import math

import jax
import jax.numpy as jnp
from jax import lax
from jax.experimental import pallas as pl
from jax.experimental.pallas import tpu as pltpu
from jax.sharding import PartitionSpec as P

F32 = jnp.float32
BF16 = jnp.bfloat16
HIDE = -1e30
VMEM = pl.BlockSpec(memory_space=pltpu.VMEM)
SMEM = pl.BlockSpec(memory_space=pltpu.SMEM)
HBM = pl.BlockSpec(memory_space=pltpu.HBM)


def iota(shape, dim):
    return lax.broadcasted_iota(jnp.int32, shape, dim)


def to_column(row):
    n = row.shape[1]
    eye = iota((n, n), 0) == iota((n, n), 1)
    return jnp.sum(jnp.where(eye, row, 0.0), axis=1, keepdims=True)


def dot_nt(a, b):
    return lax.dot_general(a, b, (((1,), (1,)), ((), ())), preferred_element_type=F32)


def merged(base_ref, kv_ref, new_ref, slot_ref, pad_ref):
    slots, tokens = kv_ref.shape[0], new_ref.shape[0]
    groups = kv_ref.shape[1] // 128
    target = jnp.where(pad_ref[...] == 1, slot_ref[...] - base_ref[0], -1).astype(F32)
    place = (iota((slots, tokens), 0).astype(F32) == target).astype(BF16)
    moved = jnp.dot(place, new_ref[...], preferred_element_type=F32)
    written = jnp.dot(place, jnp.ones((tokens, 128), BF16), preferred_element_type=F32)
    written = jnp.concatenate([written] * groups, axis=1)
    return jnp.where(written > 0.5, moved, kv_ref[...].astype(F32)).astype(BF16), target


def cache_kernel(base_ref, kv_ref, new_ref, slot_ref, pad_ref, cache_ref):
    cache_ref[...] = merged(base_ref, kv_ref, new_ref, slot_ref, pad_ref)[0]


def sort_kernel(base_ref, *refs):
    sources, rows_ref, held, arrived = refs[:6], refs[6], refs[7:13], refs[13]
    copies = [pltpu.make_async_copy(a, b, arrived.at[i]) for i, (a, b) in enumerate(zip(sources, held))]
    for copy in copies:
        copy.start()
    for copy in copies:
        copy.wait()
    kv_ref, new_ref, slot_ref, pad_ref, cseg_ref, tseg_ref = held
    slots, tokens = kv_ref.shape[0], new_ref.shape[0]
    groups = kv_ref.shape[1] // 128
    cache, target = merged(base_ref, kv_ref, new_ref, slot_ref, pad_ref)
    back = to_column(target) == iota((tokens, slots), 1).astype(F32)
    order = jnp.sum(jnp.where(back, (iota((tokens, slots), 0) + 1).astype(F32), 0.0), axis=0, keepdims=True) - 1.0
    new_seg = jnp.sum(jnp.where(back, to_column(tseg_ref[...].astype(F32)), 0.0), axis=0, keepdims=True)
    seg = jnp.where(order >= 0.0, new_seg, cseg_ref[...].astype(F32))
    lane = iota((1, slots), 1).astype(F32)
    key = jnp.where(seg < 0.0, 64.0, seg) * slots + lane
    rank = jnp.sum(jnp.where(to_column(key) < key, 1.0, 0.0), axis=0, keepdims=True)
    perm = (iota((slots, slots), 0).astype(F32) == rank).astype(BF16)
    rows = jnp.dot(perm, cache, preferred_element_type=F32).astype(BF16)
    wide = groups * 128
    lane, turn = iota((128, wide), 1), iota((128, wide), 0)
    lane = lane - (turn // 64) * 128
    turn = turn % 64
    rows_ref[:slots, :] = dot_nt(rows, (lane == turn).astype(BF16)).astype(BF16)
    rows_ref[slots : 2 * slots, :] = dot_nt(rows, (lane == turn + 64).astype(BF16)).astype(BF16)
    sub = iota((8, slots), 0)
    labels = jnp.where(sub == 0, seg, jnp.where(sub == 1, order, 0.0)).astype(BF16)
    labels = dot_nt(labels, perm)
    parts = [labels[r : r + 1, c : c + 128] for r in range(2) for c in range(0, slots, 128)]
    parts.append(jnp.zeros((16 - len(parts), 128), F32))
    rows_ref[2 * slots :, :] = jnp.concatenate(parts, axis=0).astype(BF16)


def attend_kernel(first, last, count, *refs):
    off_ref, sink_ref, seg_ref, q_ref, tseg_ref, pad_ref = refs[:6]
    rows_refs = refs[6 : 6 + count]
    given_ref, out_ref, extra_ref, *sent_ref = refs[6 + count :][: 4 if first else 3]
    q_scr, key_scr, val_scr, label_scr, row_scr, acc_scr, moved = refs[6 + count :][4 if first else 3 :]
    if first:
        load = pltpu.make_async_copy(given_ref, sent_ref[0], moved.at[0])
    else:
        load = pltpu.make_async_copy(given_ref, acc_scr, moved.at[0])
    load.start()
    extra_ref[...] = jnp.zeros_like(extra_ref)
    tokens = q_ref.shape[1]
    heads = q_ref.shape[0] // 64
    slots = (rows_refs[0].shape[0] - 16) // 2
    tiles = slots // 128
    zero = jnp.zeros((64, tokens), BF16)
    scale = jnp.array(0.125, BF16)
    for h in range(heads):
        q = q_ref[h * 64 : (h + 1) * 64, :] * scale
        pair = [q, zero] if h < heads // 2 else [zero, q]
        q_scr[:, h * tokens : (h + 1) * tokens] = jnp.concatenate(pair, axis=0)
    tseg = tseg_ref[...].astype(F32)
    tok = iota((1, tokens), 1).astype(F32)
    low, high = seg_ref[0].astype(F32), seg_ref[tokens - 1].astype(F32)
    eye = (iota((128, 128), 0) == iota((128, 128), 1)).astype(BF16)
    stretches = []
    for b in range(count):
        meta = rows_refs[b][2 * slots :, :].astype(F32)
        real = (iota((16, 128), 0) < tiles) & (meta >= 0.0)
        counts = jnp.where(real & (meta < low), 1.0, 0.0) + jnp.where(real & (meta <= high), 1024.0, 0.0)
        counts = jnp.sum(jnp.sum(counts, axis=0, keepdims=True), axis=1, keepdims=True).astype(jnp.int32)
        begin, end = (counts & 1023) >> 4, (counts >> 10) + 31 >> 4
        stretches.append(begin + (end << 6))
        for c in range(tiles):
            order = meta[tiles + c : tiles + c + 1, :]
            order = jnp.where(order < 0.0, -1.0, jnp.clip(order + off_ref[b].astype(F32), -1.0, tokens))
            label = jnp.concatenate([meta[c : c + 1, :], order, jnp.zeros((14, 128), F32)], axis=0)
            label_scr[b, c * 128 : (c + 1) * 128, :16] = dot_nt(eye, label.astype(BF16))
        label_scr[b, slots:, :16] = jnp.full((32, 16), -1.0, F32)
    packed = [stretches[b] + (stretches[b + 1] << 12) for b in range(0, count, 2)]
    packed = [jnp.sum(p) for p in packed]

    used = jnp.int32(0)
    for b in range(count):
        stretch = packed[b // 2] >> (12 * (b % 2))
        begin = stretch & 63
        steps = jnp.maximum(((stretch >> 6) & 63) - begin, 0) >> 1

        def move(i, carry, b=b, begin=begin, used=used):
            at = pl.multiple_of(begin * 16 + i * 32, 16)
            to = pl.multiple_of(used + i * 32, 32)
            key_scr[pl.ds(to, 32), :] = rows_refs[b][pl.ds(at, 32), :]
            val_scr[pl.ds(to, 32), :] = rows_refs[b][pl.ds(pl.multiple_of(slots + at, 16), 32), :]
            row_scr[pl.ds(to, 32), :] = label_scr[b, pl.ds(at, 32), :]
            return carry

        lax.fori_loop(0, steps, move, 0)
        used = used + steps * 32
    rest = pl.ds(pl.multiple_of(used, 32), 256)
    key_scr[rest, :] = jnp.zeros((256, 128), BF16)
    val_scr[rest, :] = jnp.zeros((256, 128), BF16)
    row_scr[rest, :] = jnp.full((256, 128), -1.0, F32)
    if first:
        for h in range(heads):
            span = slice(h * tokens, (h + 1) * tokens)
            acc_scr[:64, span] = jnp.zeros((64, tokens), F32)
            acc_scr[64:72, span] = jnp.ones((8, tokens), F32)
            acc_scr[72:80, span] = jnp.full((8, tokens), sink_ref[h], F32)
    else:
        load.wait()
    half = heads // 2 * tokens

    def block(at, size):
        keys = key_scr[pl.ds(at, size), :]
        rows = row_scr[pl.ds(at, size), :]
        seen = (rows[:, :1] == tseg) & (rows[:, 1:2] <= tok)
        bias = jnp.concatenate([jnp.where(seen, 0.0, HIDE)] * (heads // 2), axis=1)
        turned = dot_nt(eye, val_scr[pl.ds(at, size), :]).astype(BF16)
        ones = jnp.ones((16, size), BF16)
        spans = [slice(group * half, (group + 1) * half) for group in range(2)]
        scores = [jnp.dot(keys, q_scr[:, span], preferred_element_type=F32) + bias for span in spans]
        peaks = [acc_scr[72:73, span] for span in spans]
        tops = [jnp.maximum(jnp.max(s, axis=0, keepdims=True), p) for s, p in zip(scores, peaks)]
        weights = [jnp.exp(s - t).astype(BF16) for s, t in zip(scores, tops)]
        for group, span in enumerate(spans):
            vals = jnp.concatenate([turned[group * 64 : (group + 1) * 64, :], ones], axis=0)
            new = jnp.dot(vals, weights[group], preferred_element_type=F32)[:72, :]
            acc_scr[:72, span] = acc_scr[:72, span] * jnp.exp(peaks[group] - tops[group]) + new
            acc_scr[72:80, span] = jnp.broadcast_to(tops[group], (8, half))

    def pair(index, carry):
        block(pl.multiple_of(index * 256, 256), 256)
        return carry

    tiles_used = (used + 127) >> 7
    lax.fori_loop(0, tiles_used >> 1, pair, 0)

    @pl.when((tiles_used & 1) == 1)
    def _():
        block(pl.multiple_of((tiles_used - 1) * 128, 128), 128)

    if not last:
        save = pltpu.make_async_copy(acc_scr, out_ref, moved.at[1])
        save.start()
        save.wait()
        if first:
            load.wait()
    else:
        live = pad_ref[...].astype(F32)
        for h in range(heads):
            span = slice(h * tokens, (h + 1) * tokens)
            out_ref[h * 64 : (h + 1) * 64, :] = (acc_scr[:64, span] / acc_scr[64:65, span] * live).astype(BF16)


def attend(first, last, off, sink, q, seg, tseg, pad, rows, given):
    count = len(rows)
    width, tokens = q.shape
    heads = width // 64
    slots = (rows[0].shape[0] - 16) // 2
    if last:
        out = (jax.ShapeDtypeStruct((width, tokens), BF16), jax.ShapeDtypeStruct((1, width), BF16))
    else:
        out = (jax.ShapeDtypeStruct((80, heads * tokens), F32), jax.ShapeDtypeStruct((1, 128), BF16))
    if first:
        out += (jax.ShapeDtypeStruct(given.shape, given.dtype),)
    args = [off, sink, seg, q, tseg, pad, *rows, given]
    return pl.pallas_call(
        functools.partial(attend_kernel, first, last, count),
        out_shape=out,
        in_specs=[SMEM] * 3 + [VMEM] * (3 + count) + [HBM],
        out_specs=(VMEM if last else HBM, VMEM) + ((HBM,) if first else ()),
        scratch_shapes=[
            pltpu.VMEM((128, heads * tokens), BF16),
            pltpu.VMEM((count * slots + 256, 128), BF16),
            pltpu.VMEM((count * slots + 256, 128), BF16),
            pltpu.VMEM((count, slots + 32, 128), F32),
            pltpu.VMEM((count * slots + 256, 128), F32),
            pltpu.VMEM((80, heads * tokens), F32),
            pltpu.SemaphoreType.DMA((2,)),
        ],
        compiler_params=pltpu.CompilerParams(vmem_limit_bytes=16 * 2**20),
        cost_estimate=pl.CostEstimate(
            flops=1 * heads * tokens * slots * count * 128,
            bytes_accessed=10**6,
            transcendentals=0,
        ),
    )(*args)


def project_kernel(pos_ref, rows_ref, w0_ref, w1_ref, w2_ref, *refs):
    core, swap = pos_ref[0], pos_ref[1]
    *w3_refs, a_ref, b_ref = refs
    rows = rows_ref[...]

    def block(one, two):
        a = [jnp.dot(one[...], rows, preferred_element_type=F32)]
        b = [jnp.dot(w[...], rows, preferred_element_type=F32) for w in two]
        return jnp.where(core == 0, jnp.concatenate(a + b, axis=0), jnp.concatenate(b + a, axis=0)).astype(BF16)

    here, there = block(w0_ref, [w1_ref]), block(w2_ref, w3_refs)
    a_ref[...] = jnp.where(swap == 0, here, there)
    b_ref[...] = jnp.where(swap == 0, there, here)


def tuned(queries, new_kv, kv_cache, cache_seg, cache_slot, token_seg, pad_mask, sink_logits, out_weight, out_bias):
    tokens, slots = queries.shape[0], kv_cache.shape[0]
    groups = kv_cache.shape[1]
    plane, own = lax.axis_index("gx"), lax.axis_index("gy")
    core, x, y = own % 2, (own // 2) % 2, own // 4

    def gy(value, m):
        return lax.ppermute(value, "gy", [(i, i ^ m) for i in range(8)])

    def gx(value, m):
        return lax.ppermute(value, "gx", [(i, i ^ m) for i in range(4)])

    tseg, pad = token_seg.reshape(1, tokens), pad_mask.reshape(1, tokens)
    store = [
        (own * slots).reshape(1).astype(jnp.int32),
        kv_cache.reshape(slots, groups * 128),
        new_kv.reshape(tokens, groups * 128),
        cache_slot.reshape(1, tokens),
        pad,
    ]
    rows = pl.pallas_call(
        sort_kernel,
        out_shape=jax.ShapeDtypeStruct((groups * slots + 16, 128), BF16),
        in_specs=[SMEM] + [HBM] * 6,
        out_specs=VMEM,
        scratch_shapes=[
            pltpu.VMEM((slots, groups * 128), BF16),
            pltpu.VMEM((tokens, groups * 128), BF16),
            pltpu.VMEM((1, tokens), jnp.int32),
            pltpu.VMEM((1, tokens), jnp.int32),
            pltpu.VMEM((1, slots), jnp.int32),
            pltpu.VMEM((1, tokens), jnp.int32),
            pltpu.SemaphoreType.DMA((6,)),
        ],
        compiler_params=pltpu.CompilerParams(vmem_limit_bytes=16 * 2**20),
    )(*store, cache_seg.reshape(1, slots), tseg)

    rows_x = gy(rows, 2)
    rows_y = gy(rows, 4)
    near = [rows, gy(rows, 1)]
    w0 = out_weight.T

    def offsets(m):
        return jnp.stack([((own ^ m) - own) * tokens, ((own ^ m ^ 1) - own) * tokens]).astype(jnp.int32)

    turned = queries.T
    step = functools.partial(attend, sink=sink_logits, q=turned, seg=token_seg, tseg=tseg, pad=pad)
    state, zeros, sent = step(True, False, offsets(0), rows=near, given=w0)
    rows_x = rows_x + zeros
    rows_d = gy(rows_x, 4)
    w2 = gy(sent, 2)
    along = [rows_x, gy(rows_x, 1), rows_y, gy(rows_y, 1)]
    both = jnp.concatenate([offsets(2), offsets(4)])
    state, zeros = step(False, False, both, rows=along, given=state)
    w1 = gy(sent, 1)
    rows_d = rows_d + zeros
    diagonal = [rows_d, gy(rows_d, 1)]
    attention, zeros = step(False, True, offsets(6), rows=diagonal, given=state)
    other = gy(attention, 4)
    third = w2.shape[0] // 3
    w3 = [gy(w2[i * third : (i + 1) * third] + zeros, 1) for i in range(3)]

    part = jax.ShapeDtypeStruct((out_weight.shape[1] * 2, tokens), BF16)
    pos = jnp.stack([core, jnp.where(x == 1 - plane % 2, 0, 1)]).astype(jnp.int32)
    project = pl.pallas_call(
        project_kernel,
        out_shape=(part, part),
        in_specs=[SMEM] + [VMEM] * 7,
        out_specs=(VMEM, VMEM),
        compiler_params=pltpu.CompilerParams(vmem_limit_bytes=16 * 2**20),
        cost_estimate=pl.CostEstimate(flops=2 * 1024 * 1440 * 256, bytes_accessed=4 * 2**20, transcendentals=0),
    )
    keep_a, keep_b = project(pos, attention, w0, w1, w2, *w3)
    got_k = gx(keep_a, 1)
    send_a, send_b = project(pos, other, w0, w1, w2, *w3)
    got_s = gx(send_a, 1)
    got = gy((send_b.astype(F32) + got_s.astype(F32)).astype(BF16), 4)
    cache = pl.pallas_call(
        cache_kernel,
        out_shape=jax.ShapeDtypeStruct((slots, groups * 128), BF16),
        in_specs=[SMEM] + [VMEM] * 4,
        out_specs=VMEM,
        compiler_params=pltpu.CompilerParams(vmem_limit_bytes=16 * 2**20),
    )(*store)
    mine = keep_b.astype(F32) + got_k.astype(F32)
    theirs = got.astype(F32)
    same = y == plane // 2
    final = jnp.where(same, mine, theirs)
    away = jnp.where(same, theirs, mine).astype(BF16)
    last = gx(away, 2)
    out = (final + last.astype(F32) + out_bias[:, None]).astype(BF16)
    return out.T, cache.reshape(slots, groups, 128)


def plain(queries, new_kv, kv_cache, cache_seg, cache_slot, token_seg, pad_mask, sink_logits, out_weight, out_bias):
    local_tokens = queries.shape[0]
    local_slots = kv_cache.shape[0]
    local_groups = kv_cache.shape[1]
    head_dim = kv_cache.shape[2] // 2
    group_heads = queries.shape[1] // (local_groups * head_dim)
    scale = head_dim ** (-0.5)
    own_index = lax.axis_index("gy")
    first_token = own_index * local_tokens
    live_rows = pad_mask == 1
    target = jnp.where(live_rows, cache_slot - own_index * local_slots, local_slots)
    cache_out = kv_cache.at[target].set(new_kv, mode="drop")
    token_index = first_token + jnp.arange(local_tokens, dtype=jnp.int32)
    slot_seg = cache_seg.at[target].set(token_seg, mode="drop")
    slot_order = jnp.full((local_slots,), -1, jnp.int32).at[target].set(token_index, mode="drop")
    sink_table = sink_logits.reshape(local_groups, group_heads)
    query_heads = queries.reshape(local_tokens, local_groups, group_heads, head_dim)
    initial = (
        jnp.broadcast_to(sink_table[:, :, None], (local_groups, group_heads, local_tokens)),
        jnp.ones((local_groups, group_heads, local_tokens), jnp.float32),
        jnp.zeros((local_groups, group_heads, local_tokens, head_dim), jnp.float32),
    )
    kv_rows = lax.all_gather(cache_out, "gy", axis=0, tiled=True)
    seg_rows = lax.all_gather(slot_seg, "gy", axis=0, tiled=True)
    order_rows = lax.all_gather(slot_order, "gy", axis=0, tiled=True)
    total_rows = kv_rows.shape[0]
    blk_rows = math.gcd(total_rows, 512)
    count_blocks = total_rows // blk_rows
    stacked = (
        kv_rows.reshape(count_blocks, blk_rows, local_groups, 2 * head_dim),
        seg_rows.reshape(count_blocks, blk_rows),
        order_rows.reshape(count_blocks, blk_rows),
    )

    def one_block(running, block_data):
        run_peak, weight_sum, weighted = running
        block_kv, block_seg, block_order = block_data
        visible = (block_seg[None, :] == token_seg[:, None]) & (block_order[None, :] <= token_index[:, None])
        scores = (
            jnp.einsum("tgqd,cgd->gqtc", query_heads, block_kv[:, :, :head_dim], preferred_element_type=jnp.float32)
            * scale
        )
        new_peak = jnp.maximum(run_peak, jnp.max(jnp.where(visible, scores, -jnp.inf), axis=-1))
        rescale = jnp.exp(run_peak - new_peak)
        weights = jnp.where(visible, jnp.exp(scores - new_peak[..., None]), 0.0)
        weight_sum = weight_sum * rescale + jnp.sum(weights, axis=-1)
        weighted = weighted * rescale[..., None] + jnp.einsum(
            "gqtc,cgd->gqtd",
            weights.astype(jnp.bfloat16),
            block_kv[:, :, head_dim:],
            preferred_element_type=jnp.float32,
        )
        return ((new_peak, weight_sum, weighted), None)

    result, unused = lax.scan(one_block, initial, stacked)
    run_peak, weight_sum, weighted = result
    attn_heads = jnp.transpose(weighted / weight_sum[..., None], (2, 0, 1, 3)).reshape(
        local_tokens, local_groups * group_heads * head_dim
    )
    attention = (attn_heads * pad_mask[:, None].astype(jnp.float32)).astype(jnp.bfloat16)
    partial_out = jnp.dot(
        attention, lax.all_gather(out_weight, "gy", axis=1, tiled=True), preferred_element_type=jnp.float32
    )
    summed = lax.psum_scatter(
        partial_out.astype(jnp.bfloat16), "gx", scatter_dimension=1, tiled=True
    ).astype(jnp.float32)
    return ((summed + out_bias).astype(jnp.bfloat16), cache_out)


def solution(mesh):
    placed = (
        P("gy", "gx"),
        P("gy", "gx", None),
        P("gy", "gx", None),
        P("gy"),
        P("gy"),
        P("gy"),
        P("gy"),
        P("gx"),
        P("gx", "gy"),
        P("gx"),
    )
    small = mesh.shape["gy"] == 8 and mesh.shape["gx"] == 4
    return jax.shard_map(
        tuned if small else plain,
        mesh=mesh,
        in_specs=placed,
        out_specs=(P("gy", "gx"), P("gy", "gx", None)),
        check_vma=False,
    )
```
